32 devices in a mesh: wide: 16 (over z, x, core), narrow: 2 (over y).
Axes of the slice: x: 2, y: 2, z: 4, core: 2. Of those that a mesh axis runs over, the one named last changes fastest.
Arguments:
- fields: bfloat16 [2, 512, 64, 1024], P(None, 'wide', 'narrow'), may hold values from -6 to 6
- vel_x: float32 [512], P('wide'), may hold values from -1 to 1
- vel_y: float32 [512], P('wide'), may hold values from -1 to 1
- collision: bfloat16 [1024, 1024], replicated, may hold values from -1 to 2
Outputs:
- smoothed: bfloat16 [2, 512, 64, 1024], P(None, 'wide', 'narrow')
The draws below stay inside these ranges and needn't reach their ends.
All inputs are finite; a program needn't handle non-finite values.
Results may differ from the reference program's by a relative error of at most 0.001.
The reference program's roundings to bfloat16 on the way count: a program that leaves them out, or rounds other values in their place, can miss the bound.
Values may be sent and summed in bfloat16 or wider, within the bound.
A program may use at most 192 MiB of HBM per device.

```python
import jax
import jax.numpy as jnp
import numpy as np
from jax import lax

V = 512
FIELDS = 2
NODES = 64
EY = 16
EX = 64


def draw_collision(key, part):
    extent = 2 * V
    random_part = jax.random.truncated_normal(key, -4.0, 4.0, (extent, extent), jnp.float32)
    matrix = jnp.eye(extent, dtype=jnp.float32) + 0.5 * random_part / jnp.sqrt(jnp.float32(extent))
    return matrix.astype(jnp.bfloat16)


def levels(stream_key, dims, split, smallest, top_value):
    loudness = 1.0
    for axis_at, shards_of in split:
        steps = jax.random.uniform(jax.random.fold_in(jax.random.fold_in(stream_key, 6), axis_at), (shards_of,), jnp.float32, smallest / len(split), top_value / len(split))
        loudness = loudness * jnp.repeat(jnp.exp(steps), dims[axis_at] // shards_of).reshape((-1,) + (1,) * (len(dims) - 1 - axis_at))
    return loudness


def bell_draw(rng, shape, scale, bound, split=(), held_as=jnp.bfloat16):
    values = jax.random.normal(rng, shape, jnp.float32) * scale
    if len(split) > 0:
        values = levels(rng, shape, split, -0.22, 0.18) * values
    return jnp.clip(values, min=-bound, max=bound).astype(held_as)


def setup_inputs(seed: int = 0) -> dict:
    key_of = jax.random.split(jax.random.key(seed), 5)
    return {
        "fields": bell_draw(key_of[0], (FIELDS, V, EX, EY * NODES), 1.0, 6.0, ((1, 16), (2, 2))),
        "vel_x": jnp.clip(jax.random.uniform(key_of[1], (V,), jnp.float32, -1.0, 1.0) * levels(key_of[1], (V,), ((0, 16),), -0.4, 0.0), -1.0, 1.0),
        "vel_y": jnp.clip(jax.random.uniform(key_of[2], (V,), jnp.float32, -1.0, 1.0) * levels(key_of[2], (V,), ((0, 16),), -0.4, 0.0), -1.0, 1.0),
        "collision": draw_collision(jax.random.fold_in(key_of[4], 71), 0),
    }


time_step = 0.02
lift_gain = 24.0
upwind_share = 0.5


def volume_table():
    points_ref = -np.cos(np.pi * np.arange(8) / 7.0)
    identity = np.eye(8)
    differ = points_ref[:, None] - points_ref[None, :] + identity
    weights = 1.0 / np.prod(differ, axis=1)
    derivative = (weights[None, :] / weights[:, None]) / differ * (1.0 - identity)
    derivative = derivative - identity * derivative.sum(axis=1)[:, None]
    along_x = np.kron(np.eye(2), np.kron(derivative, np.eye(8)))
    along_y = np.kron(np.eye(2), np.kron(np.eye(8), derivative))
    joined = np.concatenate([along_x.T, along_y.T], axis=1)
    return jnp.asarray(joined, dtype=jnp.float32).astype(jnp.bfloat16)


def sweep(current, speed_x, speed_y, from_prev, from_next, table):
    shape = current.shape
    lanes = shape[3]
    pairs = current.reshape(shape[0], shape[1], shape[2], lanes // 128, 128)
    slopes = jnp.dot(pairs, table, preferred_element_type=jnp.float32)
    grad_x = slopes[..., :128].reshape(shape)
    grad_y = slopes[..., 128:].reshape(shape)
    values = current.astype(jnp.float32)
    index = lax.iota(jnp.int32, lanes)
    node_p = (index // 8) % 8
    node_q = index % 8
    first_p = (node_p == 0).astype(jnp.float32)
    last_p = (node_p == 7).astype(jnp.float32)
    first_q = (node_q == 0).astype(jnp.float32)
    last_q = (node_q == 7).astype(jnp.float32)
    below = jnp.roll(values, 57, axis=3)
    above = jnp.roll(values, -57, axis=3)
    coef_x = speed_x[:, :, None, None]
    coef_y = speed_y[:, :, None, None]
    plus_x = 0.5 * (coef_x + upwind_share * jnp.abs(coef_x))
    minus_x = 0.5 * (coef_x - upwind_share * jnp.abs(coef_x))
    plus_y = 0.5 * (coef_y + upwind_share * jnp.abs(coef_y))
    minus_y = 0.5 * (coef_y - upwind_share * jnp.abs(coef_y))
    change_x = -coef_x * grad_x + lift_gain * (minus_x * last_p * (values - from_next) + plus_x * first_p * (from_prev - values))
    change_y = -coef_y * grad_y + lift_gain * (minus_y * last_q * (values - above) + plus_y * first_q * (below - values))
    return (values + time_step * (change_x + change_y)).astype(jnp.bfloat16)


def reference(fields, vel_x, vel_y, collision):
    table = volume_table()
    signs = jnp.array([1.0, -1.0], jnp.float32)
    blocks = V // 16
    lanes = EY * 64
    grouped = fields.reshape(2, blocks, 16, EX, lanes).transpose(1, 0, 2, 3, 4)
    speeds_x = vel_x.reshape(blocks, 16)
    speeds_y = vel_y.reshape(blocks, 16)

    def one_block(items):
        current, along_x, along_y = items
        values = current.astype(jnp.float32)
        from_prev = jnp.roll(jnp.roll(values, -56, axis=3), 1, axis=2)
        from_next = jnp.roll(jnp.roll(values, 56, axis=3), -1, axis=2)
        return sweep(current, signs[:, None] * along_x[None, :], signs[:, None] * along_y[None, :], from_prev, from_next, table)

    moved = lax.map(one_block, (grouped, speeds_x, speeds_y))
    moved = moved.transpose(1, 0, 2, 3, 4).reshape(2 * V, EX, lanes)

    def one_column(column):
        return jnp.dot(collision, column, preferred_element_type=jnp.float32).astype(jnp.bfloat16)

    mixed = lax.map(one_column, moved.transpose(1, 0, 2))
    return mixed.transpose(1, 0, 2).reshape(2, V, EX, lanes)
```

```python
import functools

import jax
import jax.numpy as jnp
import numpy as np
from jax import lax
from jax.experimental import pallas as pl
from jax.experimental.pallas import tpu as pltpu
from jax.sharding import PartitionSpec as P

time_step = 0.02
lift_gain = 24.0
upwind_share = 0.5
GROUP = 16
CHUNK = 128
TILE = 256
MESH = pl.DeviceIdType.MESH


def derivative_matrix():
    points_ref = -np.cos(np.pi * np.arange(8) / 7.0)
    identity = np.eye(8)
    differ = points_ref[:, None] - points_ref[None, :] + identity
    weights = 1.0 / np.prod(differ, axis=1)
    derivative = weights[None, :] / weights[:, None] / differ * (1.0 - identity)
    return derivative - identity * derivative.sum(axis=1)[:, None]


def as_table(matrix):
    return jnp.asarray(matrix, dtype=jnp.float32).astype(jnp.bfloat16)


def lane_tables():
    derivative = derivative_matrix()
    along_x = np.kron(np.eye(2), np.kron(derivative, np.eye(8)))
    along_y = np.kron(np.eye(2), np.kron(np.eye(8), derivative))
    slopes = np.concatenate([along_x.T, along_y.T], axis=1)
    lane = np.arange(CHUNK)
    p, q = lane // 8 % 8, lane % 8
    faces_x = np.zeros((2 * CHUNK, CHUNK))
    first, last = lane[p == 0], lane[p == 7]
    faces_x[first + 56, first] = 1.0
    faces_x[CHUNK + last - 56, last] = 1.0
    faces_y = np.zeros((3 * CHUNK, CHUNK))
    for target in lane[q == 0]:
        source = target - 57
        faces_y[source if source >= 0 else 2 * CHUNK + source, target] = 1.0
    for target in lane[q == 7]:
        source = target + 57
        faces_y[source if source < CHUNK else CHUNK + source, target] = 1.0
    return as_table(slopes), as_table(faces_x), as_table(faces_y)


def swap_table():
    row = np.arange(GROUP * GROUP)
    table = np.zeros((GROUP * GROUP, GROUP * GROUP))
    table[row, row % GROUP * GROUP + row // GROUP] = 1.0
    return as_table(table)


def restore_table(each):
    owners = GROUP // each
    v, column = np.meshgrid(np.arange(GROUP), np.arange(GROUP), indexing="ij")
    source = (column % each * owners + column // each) * GROUP + v
    table = np.zeros((GROUP * GROUP, GROUP * GROUP))
    table[(v * GROUP + column).ravel(), source.ravel()] = 1.0
    return as_table(table)


def sweep_kernel(
    n, strips, each,
    fields, vel_x, vel_y, collision, slopes, faces_x, faces_y, swap,
    result,
    columns, packed, gathered, mixed, coefs,
    edge_send, edge_recv, out_send, out_recv, back_send, back_recv, own_sem,
):
    me = lax.axis_index("wide")
    strip = lax.axis_index("narrow")
    pairs, local, width, lanes = fields.shape
    rows = pairs * local
    speeds = n * local
    chunks = lanes // CHUNK
    above, below = lax.rem(strip + 1, strips), lax.rem(strip + strips - 1, strips)

    barrier = pltpu.get_barrier_semaphore()

    def greet(i, carry):
        pl.semaphore_signal(
            barrier, inc=1, device_id={"wide": lax.rem(me + i, n)}, device_id_type=MESH
        )
        return carry

    lax.fori_loop(1, n, greet, 0)
    for neighbour in (above, below):
        pl.semaphore_signal(barrier, inc=1, device_id={"narrow": neighbour}, device_id_type=MESH)

    for s in range(pairs):
        for g in range(local // GROUP):
            def turn(h, carry):
                at = pl.multiple_of(h * GROUP, GROUP)
                for t in range(lanes // TILE):
                    part = pl.ds(t * TILE, TILE)
                    block = fields[s, pl.ds(g * GROUP, GROUP), pl.ds(at, GROUP), part]
                    turned = jnp.dot(
                        swap[...], block.reshape(GROUP * GROUP, TILE),
                        preferred_element_type=jnp.float32,
                    )
                    columns[
                        pl.ds(at + 1, GROUP), pl.ds(s * local + g * GROUP, GROUP), part
                    ] = turned.astype(jnp.bfloat16).reshape(GROUP, GROUP, TILE)
                return carry

            lax.fori_loop(0, width // GROUP, turn, 0)

    lane = lax.broadcasted_iota(jnp.int32, (rows, CHUNK), 1)
    node_p = (lane >> 3) & 7
    node_q = lane & 7
    eye = lax.broadcasted_iota(jnp.int32, (local, local), 0) == lax.broadcasted_iota(
        jnp.int32, (local, local), 1
    )

    def signed(vel):
        spread = jnp.broadcast_to(vel[...], (local, local))
        column = jnp.sum(jnp.where(eye, spread, 0.0), axis=1, keepdims=True)
        return jnp.broadcast_to(jnp.concatenate([column, -column], axis=0), (rows, CHUNK))

    lift = time_step * lift_gain
    own = jnp.ones((rows, CHUNK), jnp.float32)
    for k, (speed, node) in enumerate(((signed(vel_x), node_p), (signed(vel_y), node_q))):
        plus = 0.5 * (speed + upwind_share * jnp.abs(speed))
        minus = 0.5 * (speed - upwind_share * jnp.abs(speed))
        face = lift * (jnp.where(node == 0, plus, 0.0) - jnp.where(node == 7, minus, 0.0))
        own = own - face
        coefs[1 + k] = -time_step * speed
        coefs[3 + k] = face
    coefs[0] = own

    pl.semaphore_wait(barrier, n + 1)

    def edge(k):
        source, target, device = ((width, 0, above), (1, width + 1, below))[k]
        return pltpu.make_async_remote_copy(
            src_ref=columns.at[source], dst_ref=columns.at[target],
            send_sem=edge_send.at[k], recv_sem=edge_recv.at[k],
            device_id={"narrow": device}, device_id_type=MESH,
        )

    edge(0).start()
    edge(1).start()

    def outward(c, d, at):
        return pltpu.make_async_remote_copy(
            src_ref=packed.at[c, d],
            dst_ref=gathered.at[c, :, pl.ds(pl.multiple_of(at * local, GROUP), local), :],
            send_sem=out_send.at[c, d], recv_sem=out_recv.at[c, at],
            device_id={"wide": d}, device_id_type=MESH,
        )

    def stacked(value, shift):
        return jnp.concatenate(
            [
                value[:, (m + shift) % chunks * CHUNK : ((m + shift) % chunks + 1) * CHUNK]
                for m in range(chunks)
            ],
            axis=0,
        )

    for c in range(each):
        def transport(i, carry):
            d = lax.rem(me + i, n)
            if c == 0:
                @pl.when(d == 0)
                def _():
                    edge(0).wait_recv()
            if c == each - 1:
                @pl.when(d == n - 1)
                def _():
                    edge(1).wait_recv()
            j = d * each + c
            now = columns[j + 1]
            here = stacked(now, 0)
            slope = jnp.dot(here, slopes[...], preferred_element_type=jnp.float32)
            next_x = jnp.dot(
                jnp.concatenate([stacked(columns[j], 0), stacked(columns[j + 2], 0)], axis=1),
                faces_x[...], preferred_element_type=jnp.float32,
            )
            next_y = jnp.dot(
                jnp.concatenate([here, stacked(now, -1), stacked(now, 1)], axis=1),
                faces_y[...], preferred_element_type=jnp.float32,
            )
            for m in range(chunks):
                span = slice(m * rows, (m + 1) * rows)
                moved = (
                    coefs[0] * here[span].astype(jnp.float32)
                    + coefs[1] * slope[span, :CHUNK]
                    + coefs[2] * slope[span, CHUNK:]
                    + coefs[3] * next_x[span]
                    + coefs[4] * next_y[span]
                )
                packed[c, d, :, :, pl.ds(m * CHUNK, CHUNK)] = moved.astype(jnp.bfloat16).reshape(
                    pairs, local, CHUNK
                )

            @pl.when(i < n)
            def _():
                outward(c, d, me).start()

            return carry

        lax.fori_loop(1, n + 1, transport, 0)
        pltpu.make_async_copy(
            packed.at[c, me],
            gathered.at[c, :, pl.ds(pl.multiple_of(me * local, GROUP), local), :],
            own_sem.at[c],
        ).start()

    def back(c, d, at):
        return pltpu.make_async_remote_copy(
            src_ref=mixed.at[c, d], dst_ref=result.at[c, at],
            send_sem=back_send.at[c, d], recv_sem=back_recv.at[c, at],
            device_id={"wide": d}, device_id_type=MESH,
        )

    for c in range(each):
        pltpu.make_async_copy(
            packed.at[c, me],
            gathered.at[c, :, pl.ds(pl.multiple_of(me * local, GROUP), local), :],
            own_sem.at[c],
        ).wait()

        def arrive(i, carry):
            d = lax.rem(me + n - i, n)
            outward(c, d, d).wait_recv()
            return carry

        lax.fori_loop(1, n, arrive, 0)

        def collide(i, carry):
            d = lax.rem(me + i, n)
            left = jnp.concatenate(
                [
                    collision[pl.ds(pl.multiple_of(s * speeds + d * local, GROUP), local), :]
                    for s in range(pairs)
                ],
                axis=0,
            )
            for t in range(lanes // TILE):
                part = pl.ds(t * TILE, TILE)
                total = jnp.dot(
                    left, gathered[c, :, :, part].reshape(pairs * speeds, TILE),
                    preferred_element_type=jnp.float32,
                )
                mixed[c, d, :, :, part] = total.astype(jnp.bfloat16).reshape(pairs, local, TILE)

            @pl.when(i < n)
            def _():
                back(c, d, me).start()

            return carry

        lax.fori_loop(1, n + 1, collide, 0)
        pltpu.make_async_copy(
            mixed.at[c, me], result.at[c, me], own_sem.at[each + c]
        ).start()

    edge(0).wait_send()
    edge(1).wait_send()
    for c in range(each):
        pltpu.make_async_copy(
            mixed.at[c, me], result.at[c, me], own_sem.at[each + c]
        ).wait()

        def finish(i, carry):
            d = lax.rem(me + i, n)
            outward(c, d, me).wait_send()
            back(c, d, me).wait_send()
            back(c, d, d).wait_recv()
            return carry

        lax.fori_loop(1, n, finish, 0)


def restore_kernel(restore, block, out):
    rows = GROUP * GROUP
    lanes = out.shape[-1]
    turned = jnp.dot(
        restore[...], block[...].reshape(rows, lanes), preferred_element_type=jnp.float32
    )
    out[...] = turned.astype(jnp.bfloat16).reshape(out.shape)


def shards(fields, vel_x, vel_y, collision):
    n = lax.axis_size("wide")
    strips = lax.axis_size("narrow")
    pairs, local, width, lanes = fields.shape
    each = width // n
    rows = pairs * local
    bf16 = jnp.bfloat16
    vmem = pl.BlockSpec(memory_space=pltpu.VMEM)
    dma = pltpu.SemaphoreType.DMA
    returned = pl.pallas_call(
        functools.partial(sweep_kernel, n, strips, each),
        out_shape=jax.ShapeDtypeStruct((each, n, pairs, local, lanes), bf16),
        in_specs=[vmem] * 8,
        out_specs=pl.BlockSpec(memory_space=pl.ANY),
        scratch_shapes=[
            pltpu.VMEM((width + 2, rows, lanes), bf16),
            pltpu.VMEM((each, n, pairs, local, lanes), bf16),
            pltpu.VMEM((each, pairs, n * local, lanes), bf16),
            pltpu.VMEM((each, n, pairs, local, lanes), bf16),
            pltpu.VMEM((5, rows, CHUNK), jnp.float32),
            dma((2,)),
            dma((2,)),
            dma((each, n)),
            dma((each, n)),
            dma((each, n)),
            dma((each, n)),
            dma((2 * each,)),
        ],
        compiler_params=pltpu.CompilerParams(
            collective_id=0, has_side_effects=True, vmem_limit_bytes=48 * 1024 * 1024
        ),
    )(
        fields, vel_x.reshape(1, local), vel_y.reshape(1, local), collision,
        *lane_tables(), swap_table(),
    )
    owners = GROUP // each
    return pl.pallas_call(
        restore_kernel,
        grid=(pairs, local // GROUP, width // GROUP),
        out_shape=jax.ShapeDtypeStruct(fields.shape, bf16),
        in_specs=[
            pl.BlockSpec((GROUP * GROUP, GROUP * GROUP), lambda s, g, h: (0, 0)),
            pl.BlockSpec((each, owners, 1, GROUP, lanes), lambda s, g, h: (0, h, s, g, 0)),
        ],
        out_specs=pl.BlockSpec((1, GROUP, GROUP, lanes), lambda s, g, h: (s, g, h, 0)),
        compiler_params=pltpu.CompilerParams(vmem_limit_bytes=16 * 1024 * 1024),
    )(restore_table(each), returned)


def solution(mesh):
    return jax.shard_map(
        shards,
        mesh=mesh,
        in_specs=(P(None, "wide", "narrow", None), P("wide"), P("wide"), P()),
        out_specs=P(None, "wide", "narrow", None),
        check_vma=False,
    )
```

```python
import functools

import jax
import jax.numpy as jnp
import numpy as np
from jax import lax
from jax.experimental import pallas as pl
from jax.experimental.pallas import tpu as pltpu
from jax.sharding import PartitionSpec as P

time_step = 0.02
lift_gain = 24.0
upwind_share = 0.5
GROUP = 16
CHUNK = 128
TILE = 256
MESH = pl.DeviceIdType.MESH


def derivative_matrix():
    points_ref = -np.cos(np.pi * np.arange(8) / 7.0)
    identity = np.eye(8)
    differ = points_ref[:, None] - points_ref[None, :] + identity
    weights = 1.0 / np.prod(differ, axis=1)
    derivative = weights[None, :] / weights[:, None] / differ * (1.0 - identity)
    return derivative - identity * derivative.sum(axis=1)[:, None]


def as_table(matrix):
    return jnp.asarray(matrix, dtype=jnp.float32).astype(jnp.bfloat16)


def lane_tables():
    derivative = derivative_matrix()
    along_x = np.kron(np.eye(2), np.kron(derivative, np.eye(8)))
    along_y = np.kron(np.eye(2), np.kron(np.eye(8), derivative))
    slopes = np.concatenate([along_x.T, along_y.T], axis=1)
    lane = np.arange(CHUNK)
    p, q = lane // 8 % 8, lane % 8
    faces_x = np.zeros((2 * CHUNK, CHUNK))
    first, last = lane[p == 0], lane[p == 7]
    faces_x[first + 56, first] = 1.0
    faces_x[CHUNK + last - 56, last] = 1.0
    faces_y = np.zeros((3 * CHUNK, CHUNK))
    for target in lane[q == 0]:
        source = target - 57
        faces_y[source if source >= 0 else 2 * CHUNK + source, target] = 1.0
    for target in lane[q == 7]:
        source = target + 57
        faces_y[source if source < CHUNK else CHUNK + source, target] = 1.0
    return slopes, faces_x, faces_y


def swap_table():
    row = np.arange(GROUP * GROUP)
    table = np.zeros((GROUP * GROUP, GROUP * GROUP))
    table[row, row % GROUP * GROUP + row // GROUP] = 1.0
    return table


def joined_tables():
    slopes, faces_x, faces_y = lane_tables()
    faces = np.zeros((3 * CHUNK, TILE))
    faces[:, :CHUNK] = faces_y
    faces[: 2 * CHUNK, CHUNK:] = faces_x
    return as_table(np.concatenate([swap_table(), slopes, faces], axis=0))


def restore_table(each):
    owners = GROUP // each
    v, column = np.meshgrid(np.arange(GROUP), np.arange(GROUP), indexing="ij")
    source = (column % each * owners + column // each) * GROUP + v
    table = np.zeros((GROUP * GROUP, GROUP * GROUP))
    table[(v * GROUP + column).ravel(), source.ravel()] = 1.0
    return as_table(table)


def sweep_kernel(
    n, strips, each,
    fields_in, vel_x_in, vel_y_in, collision_in, tables_in,
    result,
    fields, vel_x, vel_y, collision, tables, columns, packed, gathered, mixed, coefs,
    edge_send, edge_recv, out_send, out_recv, back_send, back_recv, own_sem, load_sem,
):
    me = lax.axis_index("wide")
    strip = lax.axis_index("narrow")
    pairs, local, width, lanes = fields.shape
    rows = pairs * local
    speeds = n * local
    chunks = lanes // CHUNK
    groups = local // GROUP
    swap = tables.at[pl.ds(0, TILE), :]
    slopes = tables.at[pl.ds(TILE, CHUNK), :]
    faces_y = tables.at[pl.ds(TILE + CHUNK, 3 * CHUNK), pl.ds(0, CHUNK)]
    faces_x = tables.at[pl.ds(TILE + CHUNK, 2 * CHUNK), pl.ds(CHUNK, CHUNK)]
    loads = [pltpu.make_async_copy(tables_in, tables, load_sem.at[0])]
    for s in range(pairs):
        for g in range(groups):
            part = (s, pl.ds(g * GROUP, GROUP))
            loads.append(
                pltpu.make_async_copy(
                    fields_in.at[part], fields.at[part], load_sem.at[1 + s * groups + g]
                )
            )
    for k, (source, target) in enumerate(
        ((vel_x_in, vel_x), (vel_y_in, vel_y), (collision_in, collision))
    ):
        loads.append(
            pltpu.make_async_copy(source, target, load_sem.at[1 + pairs * groups + k])
        )
    for load in loads:
        load.start()
    above, below = lax.rem(strip + 1, strips), lax.rem(strip + strips - 1, strips)

    half = n // 2
    upper, place = me // half, lax.rem(me, half)

    def partner(i):
        near = i // half
        return lax.rem(upper + 1 - near, 2) * half + lax.rem(place + i + near, half)

    barrier = pltpu.get_barrier_semaphore()

    def greet(i, carry):
        pl.semaphore_signal(
            barrier, inc=1, device_id={"wide": lax.rem(me + i, n)}, device_id_type=MESH
        )
        return carry

    lax.fori_loop(1, n, greet, 0)
    for neighbour in (above, below):
        pl.semaphore_signal(barrier, inc=1, device_id={"narrow": neighbour}, device_id_type=MESH)

    loads[0].wait()
    for s in range(pairs):
        for g in range(groups):
            loads[1 + s * groups + g].wait()

            def turn(h, carry):
                at = pl.multiple_of(h * GROUP, GROUP)
                for t in range(lanes // TILE):
                    part = pl.ds(t * TILE, TILE)
                    block = fields[s, pl.ds(g * GROUP, GROUP), pl.ds(at, GROUP), part]
                    turned = jnp.dot(
                        swap[...], block.reshape(GROUP * GROUP, TILE),
                        preferred_element_type=jnp.float32,
                    )
                    columns[
                        pl.ds(at + 1, GROUP), pl.ds(s * local + g * GROUP, GROUP), part
                    ] = turned.astype(jnp.bfloat16).reshape(GROUP, GROUP, TILE)
                return carry

            lax.fori_loop(0, width // GROUP, turn, 0)

    lane = lax.broadcasted_iota(jnp.int32, (rows, CHUNK), 1)
    node_p = (lane >> 3) & 7
    node_q = lane & 7
    eye = lax.broadcasted_iota(jnp.int32, (local, local), 0) == lax.broadcasted_iota(
        jnp.int32, (local, local), 1
    )

    def signed(vel):
        spread = jnp.broadcast_to(vel[...], (local, local))
        column = jnp.sum(jnp.where(eye, spread, 0.0), axis=1, keepdims=True)
        return jnp.broadcast_to(jnp.concatenate([column, -column], axis=0), (rows, CHUNK))

    loads[-3].wait()
    loads[-2].wait()
    lift = time_step * lift_gain
    own = jnp.ones((rows, CHUNK), jnp.float32)
    for k, (speed, node) in enumerate(((signed(vel_x), node_p), (signed(vel_y), node_q))):
        plus = 0.5 * (speed + upwind_share * jnp.abs(speed))
        minus = 0.5 * (speed - upwind_share * jnp.abs(speed))
        face = lift * (jnp.where(node == 0, plus, 0.0) - jnp.where(node == 7, minus, 0.0))
        own = own - face
        coefs[1 + k] = -time_step * speed
        coefs[3 + k] = face
    coefs[0] = own

    pl.semaphore_wait(barrier, n + 1)

    def edge(k):
        source, target, device = ((width, 0, above), (1, width + 1, below))[k]
        return pltpu.make_async_remote_copy(
            src_ref=columns.at[source], dst_ref=columns.at[target],
            send_sem=edge_send.at[k], recv_sem=edge_recv.at[k],
            device_id={"narrow": device}, device_id_type=MESH,
        )

    edge(0).start()
    edge(1).start()

    def outward(c, d, at):
        return pltpu.make_async_remote_copy(
            src_ref=packed.at[c, d],
            dst_ref=gathered.at[c, :, pl.ds(pl.multiple_of(at * local, GROUP), local), :],
            send_sem=out_send.at[c, d], recv_sem=out_recv.at[c, at],
            device_id={"wide": d}, device_id_type=MESH,
        )

    def stacked(value, shift):
        return jnp.concatenate(
            [
                value[:, (m + shift) % chunks * CHUNK : ((m + shift) % chunks + 1) * CHUNK]
                for m in range(chunks)
            ],
            axis=0,
        )

    for c in range(each):
        def transport(i, carry):
            d = partner(i)
            if c == 0:
                @pl.when(d == 0)
                def _():
                    edge(0).wait_recv()
            if c == each - 1:
                @pl.when(d == n - 1)
                def _():
                    edge(1).wait_recv()
            j = d * each + c
            now = columns[j + 1]
            here = stacked(now, 0)
            slope = jnp.dot(here, slopes[...], preferred_element_type=jnp.float32)
            next_x = jnp.dot(
                jnp.concatenate([stacked(columns[j], 0), stacked(columns[j + 2], 0)], axis=1),
                faces_x[...], preferred_element_type=jnp.float32,
            )
            next_y = jnp.dot(
                jnp.concatenate([here, stacked(now, -1), stacked(now, 1)], axis=1),
                faces_y[...], preferred_element_type=jnp.float32,
            )
            for m in range(chunks):
                span = slice(m * rows, (m + 1) * rows)
                moved = (
                    coefs[0] * here[span].astype(jnp.float32)
                    + coefs[1] * slope[span, :CHUNK]
                    + coefs[2] * slope[span, CHUNK:]
                    + coefs[3] * next_x[span]
                    + coefs[4] * next_y[span]
                )
                packed[c, d, :, :, pl.ds(m * CHUNK, CHUNK)] = moved.astype(jnp.bfloat16).reshape(
                    pairs, local, CHUNK
                )

            @pl.when(i < n - 1)
            def _():
                outward(c, d, me).start()

            return carry

        lax.fori_loop(0, n, transport, 0)
        pltpu.make_async_copy(
            packed.at[c, me],
            gathered.at[c, :, pl.ds(pl.multiple_of(me * local, GROUP), local), :],
            own_sem.at[c],
        ).start()

    def back(c, d, at):
        return pltpu.make_async_remote_copy(
            src_ref=mixed.at[c, d], dst_ref=result.at[c, at],
            send_sem=back_send.at[c, d], recv_sem=back_recv.at[c, at],
            device_id={"wide": d}, device_id_type=MESH,
        )

    loads[-1].wait()
    for c in range(each):
        pltpu.make_async_copy(
            packed.at[c, me],
            gathered.at[c, :, pl.ds(pl.multiple_of(me * local, GROUP), local), :],
            own_sem.at[c],
        ).wait()

        def arrive(i, carry):
            d = lax.rem(me + n - i, n)
            outward(c, d, d).wait_recv()
            return carry

        lax.fori_loop(1, n, arrive, 0)

        def collide(i, carry):
            d = partner(i)
            left = jnp.concatenate(
                [
                    collision[pl.ds(pl.multiple_of(s * speeds + d * local, GROUP), local), :]
                    for s in range(pairs)
                ],
                axis=0,
            )
            for t in range(lanes // TILE):
                part = pl.ds(t * TILE, TILE)
                total = jnp.dot(
                    left, gathered[c, :, :, part].reshape(pairs * speeds, TILE),
                    preferred_element_type=jnp.float32,
                )
                mixed[c, d, :, :, part] = total.astype(jnp.bfloat16).reshape(pairs, local, TILE)

            @pl.when(i < n - 1)
            def _():
                back(c, d, me).start()

            return carry

        lax.fori_loop(0, n, collide, 0)
        pltpu.make_async_copy(
            mixed.at[c, me], result.at[c, me], own_sem.at[each + c]
        ).start()

    edge(0).wait_send()
    edge(1).wait_send()
    for c in range(each):
        pltpu.make_async_copy(
            mixed.at[c, me], result.at[c, me], own_sem.at[each + c]
        ).wait()

        def finish(i, carry):
            d = lax.rem(me + i, n)
            outward(c, d, me).wait_send()
            back(c, d, me).wait_send()
            back(c, d, d).wait_recv()
            return carry

        lax.fori_loop(1, n, finish, 0)


def restore_kernel(restore, block, out):
    rows = GROUP * GROUP
    lanes = out.shape[-1]
    turned = jnp.dot(
        restore[...], block[...].reshape(rows, lanes), preferred_element_type=jnp.float32
    )
    out[...] = turned.astype(jnp.bfloat16).reshape(out.shape)


def shards(fields, vel_x, vel_y, collision):
    n = lax.axis_size("wide")
    strips = lax.axis_size("narrow")
    pairs, local, width, lanes = fields.shape
    each = width // n
    rows = pairs * local
    bf16 = jnp.bfloat16
    hbm = pl.BlockSpec(memory_space=pltpu.HBM)
    dma = pltpu.SemaphoreType.DMA
    returned = pl.pallas_call(
        functools.partial(sweep_kernel, n, strips, each),
        out_shape=jax.ShapeDtypeStruct((each, n, pairs, local, lanes), bf16),
        in_specs=[hbm] * 5,
        out_specs=hbm,
        scratch_shapes=[
            pltpu.VMEM(fields.shape, bf16),
            pltpu.VMEM((1, local), jnp.float32),
            pltpu.VMEM((1, local), jnp.float32),
            pltpu.VMEM(collision.shape, bf16),
            pltpu.VMEM((2 * TILE + 2 * CHUNK, TILE), bf16),
            pltpu.VMEM((width + 2, rows, lanes), bf16),
            pltpu.VMEM((each, n, pairs, local, lanes), bf16),
            pltpu.VMEM((each, pairs, n * local, lanes), bf16),
            pltpu.VMEM((each, n, pairs, local, lanes), bf16),
            pltpu.VMEM((5, rows, CHUNK), jnp.float32),
            dma((2,)),
            dma((2,)),
            dma((each, n)),
            dma((each, n)),
            dma((each, n)),
            dma((each, n)),
            dma((2 * each,)),
            dma((4 + pairs * (local // GROUP),)),
        ],
        compiler_params=pltpu.CompilerParams(
            collective_id=0, has_side_effects=True, vmem_limit_bytes=62 * 1024 * 1024
        ),
    )(
        fields, vel_x.reshape(1, local), vel_y.reshape(1, local), collision,
        joined_tables(),
    )
    owners = GROUP // each
    return pl.pallas_call(
        restore_kernel,
        grid=(pairs, local // GROUP, width // GROUP),
        out_shape=jax.ShapeDtypeStruct(fields.shape, bf16),
        in_specs=[
            pl.BlockSpec((GROUP * GROUP, GROUP * GROUP), lambda s, g, h: (0, 0)),
            pl.BlockSpec((each, owners, 1, GROUP, lanes), lambda s, g, h: (0, h, s, g, 0)),
        ],
        out_specs=pl.BlockSpec((1, GROUP, GROUP, lanes), lambda s, g, h: (s, g, h, 0)),
        compiler_params=pltpu.CompilerParams(vmem_limit_bytes=60 * 1024 * 1024),
    )(restore_table(each), returned)


def solution(mesh):
    return jax.shard_map(
        shards,
        mesh=mesh,
        in_specs=(P(None, "wide", "narrow", None), P("wide"), P("wide"), P()),
        out_specs=P(None, "wide", "narrow", None),
        check_vma=False,
    )
```

```python
import functools

import jax
import jax.numpy as jnp
import numpy as np
from jax import lax
from jax.experimental import pallas as pl
from jax.experimental.pallas import tpu as pltpu
from jax.sharding import PartitionSpec as P

time_step = 0.02
lift_gain = 24.0
upwind_share = 0.5
GROUP = 16
CHUNK = 128
TILE = 256
MESH = pl.DeviceIdType.MESH


def derivative_matrix():
    points_ref = -np.cos(np.pi * np.arange(8) / 7.0)
    identity = np.eye(8)
    differ = points_ref[:, None] - points_ref[None, :] + identity
    weights = 1.0 / np.prod(differ, axis=1)
    derivative = weights[None, :] / weights[:, None] / differ * (1.0 - identity)
    return derivative - identity * derivative.sum(axis=1)[:, None]


def as_table(matrix):
    return jnp.asarray(matrix, dtype=jnp.float32).astype(jnp.bfloat16)


def lane_tables():
    derivative = derivative_matrix()
    along_x = np.kron(np.eye(2), np.kron(derivative, np.eye(8)))
    along_y = np.kron(np.eye(2), np.kron(np.eye(8), derivative))
    slopes = np.concatenate([along_x.T, along_y.T], axis=1)
    lane = np.arange(CHUNK)
    p, q = lane // 8 % 8, lane % 8
    faces_x = np.zeros((2 * CHUNK, CHUNK))
    first, last = lane[p == 0], lane[p == 7]
    faces_x[first + 56, first] = 1.0
    faces_x[CHUNK + last - 56, last] = 1.0
    faces_y = np.zeros((3 * CHUNK, CHUNK))
    for target in lane[q == 0]:
        source = target - 57
        faces_y[source if source >= 0 else 2 * CHUNK + source, target] = 1.0
    for target in lane[q == 7]:
        source = target + 57
        faces_y[source if source < CHUNK else CHUNK + source, target] = 1.0
    return slopes, faces_x, faces_y


def swap_table():
    row = np.arange(GROUP * GROUP)
    table = np.zeros((GROUP * GROUP, GROUP * GROUP))
    table[row, row % GROUP * GROUP + row // GROUP] = 1.0
    return table


def joined_tables():
    slopes, faces_x, faces_y = lane_tables()
    faces = np.zeros((3 * CHUNK, TILE))
    faces[:, :CHUNK] = faces_y
    faces[: 2 * CHUNK, CHUNK:] = faces_x
    return as_table(np.concatenate([swap_table(), slopes, faces], axis=0))


def restore_table(each):
    owners = GROUP // each
    v, column = np.meshgrid(np.arange(GROUP), np.arange(GROUP), indexing="ij")
    source = (column % each * owners + column // each) * GROUP + v
    table = np.zeros((GROUP * GROUP, GROUP * GROUP))
    table[(v * GROUP + column).ravel(), source.ravel()] = 1.0
    return as_table(table)


def sweep_kernel(
    n, strips, each,
    fields_in, vel_x_in, vel_y_in, collision_in, tables_in,
    result,
    fields, vel_x, vel_y, collision, tables, columns, packed, gathered, mixed, coefs,
    edge_send, edge_recv, out_send, out_recv, back_send, back_recv, own_sem, load_sem,
):
    me = lax.axis_index("wide")
    strip = lax.axis_index("narrow")
    pairs, local, width, lanes = fields.shape
    rows = pairs * local
    speeds = n * local
    chunks = lanes // CHUNK
    groups = local // GROUP
    swap = tables.at[pl.ds(0, TILE), :]
    slopes = tables.at[pl.ds(TILE, CHUNK), :]
    faces_y = tables.at[pl.ds(TILE + CHUNK, 3 * CHUNK), pl.ds(0, CHUNK)]
    faces_x = tables.at[pl.ds(TILE + CHUNK, 2 * CHUNK), pl.ds(CHUNK, CHUNK)]
    loads = [pltpu.make_async_copy(tables_in, tables, load_sem.at[0])]
    for s in range(pairs):
        for g in range(groups):
            part = (s, pl.ds(g * GROUP, GROUP))
            loads.append(
                pltpu.make_async_copy(
                    fields_in.at[part], fields.at[part], load_sem.at[1 + s * groups + g]
                )
            )
    for k, (source, target) in enumerate(
        ((vel_x_in, vel_x), (vel_y_in, vel_y), (collision_in, collision))
    ):
        loads.append(
            pltpu.make_async_copy(source, target, load_sem.at[1 + pairs * groups + k])
        )
    for load in loads:
        load.start()
    above, below = lax.rem(strip + 1, strips), lax.rem(strip + strips - 1, strips)

    half = n // 2
    upper, place = me // half, lax.rem(me, half)

    def partner(i):
        near = i // half
        return lax.rem(upper + 1 - near, 2) * half + lax.rem(place + i + near, half)

    barrier = pltpu.get_barrier_semaphore()

    def greet(i, carry):
        pl.semaphore_signal(
            barrier, inc=1, device_id={"wide": lax.rem(me + i, n)}, device_id_type=MESH
        )
        return carry

    lax.fori_loop(1, n, greet, 0)
    for neighbour in (above, below):
        pl.semaphore_signal(barrier, inc=1, device_id={"narrow": neighbour}, device_id_type=MESH)

    loads[0].wait()
    for s in range(pairs):
        for g in range(groups):
            loads[1 + s * groups + g].wait()

            def turn(h, carry):
                at = pl.multiple_of(h * GROUP, GROUP)
                for t in range(lanes // TILE):
                    part = pl.ds(t * TILE, TILE)
                    block = fields[s, pl.ds(g * GROUP, GROUP), pl.ds(at, GROUP), part]
                    turned = jnp.dot(
                        swap[...], block.reshape(GROUP * GROUP, TILE),
                        preferred_element_type=jnp.float32,
                    )
                    columns[
                        pl.ds(at + 1, GROUP), pl.ds(s * local + g * GROUP, GROUP), part
                    ] = turned.astype(jnp.bfloat16).reshape(GROUP, GROUP, TILE)
                return carry

            lax.fori_loop(0, width // GROUP, turn, 0)

    lane = lax.broadcasted_iota(jnp.int32, (rows, CHUNK), 1)
    node_p = (lane >> 3) & 7
    node_q = lane & 7
    eye = lax.broadcasted_iota(jnp.int32, (local, local), 0) == lax.broadcasted_iota(
        jnp.int32, (local, local), 1
    )

    def signed(vel):
        spread = jnp.broadcast_to(vel[...], (local, local))
        column = jnp.sum(jnp.where(eye, spread, 0.0), axis=1, keepdims=True)
        return jnp.broadcast_to(jnp.concatenate([column, -column], axis=0), (rows, CHUNK))

    loads[-3].wait()
    loads[-2].wait()
    lift = time_step * lift_gain
    own = jnp.ones((rows, CHUNK), jnp.float32)
    for k, (speed, node) in enumerate(((signed(vel_x), node_p), (signed(vel_y), node_q))):
        plus = 0.5 * (speed + upwind_share * jnp.abs(speed))
        minus = 0.5 * (speed - upwind_share * jnp.abs(speed))
        face = lift * (jnp.where(node == 0, plus, 0.0) - jnp.where(node == 7, minus, 0.0))
        own = own - face
        coefs[1 + k] = -time_step * speed
        coefs[3 + k] = face
    coefs[0] = own

    pl.semaphore_wait(barrier, n + 1)

    def edge(k):
        source, target, device = ((width, 0, above), (1, width + 1, below))[k]
        return pltpu.make_async_remote_copy(
            src_ref=columns.at[source], dst_ref=columns.at[target],
            send_sem=edge_send.at[k], recv_sem=edge_recv.at[k],
            device_id={"narrow": device}, device_id_type=MESH,
        )

    edge(0).start()
    edge(1).start()

    def outward(c, d, at):
        return pltpu.make_async_remote_copy(
            src_ref=packed.at[c, d],
            dst_ref=gathered.at[c, :, pl.ds(pl.multiple_of(at * local, GROUP), local), :],
            send_sem=out_send.at[c, d], recv_sem=out_recv.at[c, at],
            device_id={"wide": d}, device_id_type=MESH,
        )

    def stacked(value, shift):
        return jnp.concatenate(
            [
                value[:, (m + shift) % chunks * CHUNK : ((m + shift) % chunks + 1) * CHUNK]
                for m in range(chunks)
            ],
            axis=0,
        )

    for c in range(each):
        def transport(i, carry):
            d = partner(i)
            if c == 0:
                @pl.when(d == 0)
                def _():
                    edge(0).wait_recv()
            if c == each - 1:
                @pl.when(d == n - 1)
                def _():
                    edge(1).wait_recv()
            j = d * each + c
            now = columns[j + 1]
            here = stacked(now, 0)
            slope = jnp.dot(here, slopes[...], preferred_element_type=jnp.float32)
            next_x = jnp.dot(
                jnp.concatenate([stacked(columns[j], 0), stacked(columns[j + 2], 0)], axis=1),
                faces_x[...], preferred_element_type=jnp.float32,
            )
            next_y = jnp.dot(
                jnp.concatenate([here, stacked(now, -1), stacked(now, 1)], axis=1),
                faces_y[...], preferred_element_type=jnp.float32,
            )
            for m in range(chunks):
                span = slice(m * rows, (m + 1) * rows)
                moved = (
                    coefs[0] * here[span].astype(jnp.float32)
                    + coefs[1] * slope[span, :CHUNK]
                    + coefs[2] * slope[span, CHUNK:]
                    + coefs[3] * next_x[span]
                    + coefs[4] * next_y[span]
                )
                packed[c, d, :, :, pl.ds(m * CHUNK, CHUNK)] = moved.astype(jnp.bfloat16).reshape(
                    pairs, local, CHUNK
                )

            @pl.when(i < n - 1)
            def _():
                outward(c, d, me).start()

            return carry

        lax.fori_loop(0, n, transport, 0)
        pltpu.make_async_copy(
            packed.at[c, me],
            gathered.at[c, :, pl.ds(pl.multiple_of(me * local, GROUP), local), :],
            own_sem.at[c],
        ).start()

    def back(c, d, at):
        return pltpu.make_async_remote_copy(
            src_ref=mixed.at[c, d], dst_ref=result.at[c, at],
            send_sem=back_send.at[c, d], recv_sem=back_recv.at[c, at],
            device_id={"wide": d}, device_id_type=MESH,
        )

    loads[-1].wait()
    for c in range(each):
        pltpu.make_async_copy(
            packed.at[c, me],
            gathered.at[c, :, pl.ds(pl.multiple_of(me * local, GROUP), local), :],
            own_sem.at[c],
        ).wait()

        def arrive(i, carry):
            d = lax.rem(me + n - i, n)
            outward(c, d, d).wait_recv()
            return carry

        lax.fori_loop(1, n, arrive, 0)

        def collide(i, carry):
            d = partner(i)
            left = jnp.concatenate(
                [
                    collision[pl.ds(pl.multiple_of(s * speeds + d * local, GROUP), local), :]
                    for s in range(pairs)
                ],
                axis=0,
            )
            for t in range(lanes // TILE):
                part = pl.ds(t * TILE, TILE)
                total = jnp.dot(
                    left, gathered[c, :, :, part].reshape(pairs * speeds, TILE),
                    preferred_element_type=jnp.float32,
                )
                mixed[c, d, :, :, part] = total.astype(jnp.bfloat16).reshape(pairs, local, TILE)

            @pl.when(i < n - 1)
            def _():
                back(c, d, me).start()

            return carry

        lax.fori_loop(0, n, collide, 0)
        pltpu.make_async_copy(
            mixed.at[c, me], result.at[c, me], own_sem.at[each + c]
        ).start()

    edge(0).wait_send()
    edge(1).wait_send()
    for c in range(each):
        pltpu.make_async_copy(
            mixed.at[c, me], result.at[c, me], own_sem.at[each + c]
        ).wait()

        def finish(i, carry):
            d = lax.rem(me + i, n)
            outward(c, d, me).wait_send()
            back(c, d, me).wait_send()
            back(c, d, d).wait_recv()
            return carry

        lax.fori_loop(1, n, finish, 0)


def restore_kernel(table_in, returned, result, table, held, turned, table_sem, in_sem, out_sem):
    each, n, pairs, local, lanes = held.shape
    owners = GROUP // each
    blocks = [
        (s, g, h)
        for s in range(pairs)
        for g in range(local // GROUP)
        for h in range(n // owners)
    ]

    def fetch(k):
        s, g, h = blocks[k]
        part = (slice(None), pl.ds(h * owners, owners), s, pl.ds(g * GROUP, GROUP))
        return pltpu.make_async_copy(returned.at[part], held.at[part], in_sem.at[k])

    def place(k):
        s, g, h = blocks[k]
        part = (s, pl.ds(g * GROUP, GROUP), pl.ds(h * GROUP, GROUP))
        return pltpu.make_async_copy(turned.at[part], result.at[part], out_sem.at[k])

    load = pltpu.make_async_copy(table_in, table, table_sem)
    load.start()
    for k in range(len(blocks)):
        fetch(k).start()
    load.wait()
    for k, (s, g, h) in enumerate(blocks):
        fetch(k).wait()
        for t in range(lanes // TILE):
            part = pl.ds(t * TILE, TILE)
            block = held[:, pl.ds(h * owners, owners), s, pl.ds(g * GROUP, GROUP), part]
            rows = jnp.dot(
                table[...], block.reshape(GROUP * GROUP, TILE),
                preferred_element_type=jnp.float32,
            )
            turned[s, pl.ds(g * GROUP, GROUP), pl.ds(h * GROUP, GROUP), part] = rows.astype(
                jnp.bfloat16
            ).reshape(GROUP, GROUP, TILE)
        place(k).start()
    for k in range(len(blocks)):
        place(k).wait()


def shards(fields, vel_x, vel_y, collision):
    n = lax.axis_size("wide")
    strips = lax.axis_size("narrow")
    pairs, local, width, lanes = fields.shape
    each = width // n
    rows = pairs * local
    bf16 = jnp.bfloat16
    hbm = pl.BlockSpec(memory_space=pltpu.HBM)
    dma = pltpu.SemaphoreType.DMA
    returned = pl.pallas_call(
        functools.partial(sweep_kernel, n, strips, each),
        out_shape=jax.ShapeDtypeStruct((each, n, pairs, local, lanes), bf16),
        in_specs=[hbm] * 5,
        out_specs=hbm,
        scratch_shapes=[
            pltpu.VMEM(fields.shape, bf16),
            pltpu.VMEM((1, local), jnp.float32),
            pltpu.VMEM((1, local), jnp.float32),
            pltpu.VMEM(collision.shape, bf16),
            pltpu.VMEM((2 * TILE + 2 * CHUNK, TILE), bf16),
            pltpu.VMEM((width + 2, rows, lanes), bf16),
            pltpu.VMEM((each, n, pairs, local, lanes), bf16),
            pltpu.VMEM((each, pairs, n * local, lanes), bf16),
            pltpu.VMEM((each, n, pairs, local, lanes), bf16),
            pltpu.VMEM((5, rows, CHUNK), jnp.float32),
            dma((2,)),
            dma((2,)),
            dma((each, n)),
            dma((each, n)),
            dma((each, n)),
            dma((each, n)),
            dma((2 * each,)),
            dma((4 + pairs * (local // GROUP),)),
        ],
        compiler_params=pltpu.CompilerParams(
            collective_id=0, has_side_effects=True, vmem_limit_bytes=62 * 1024 * 1024
        ),
    )(
        fields, vel_x.reshape(1, local), vel_y.reshape(1, local), collision,
        joined_tables(),
    )
    blocks = pairs * (local // GROUP) * (width // GROUP)
    return pl.pallas_call(
        restore_kernel,
        out_shape=jax.ShapeDtypeStruct(fields.shape, bf16),
        in_specs=[hbm] * 2,
        out_specs=hbm,
        scratch_shapes=[
            pltpu.VMEM((GROUP * GROUP, GROUP * GROUP), bf16),
            pltpu.VMEM((each, n, pairs, local, lanes), bf16),
            pltpu.VMEM(fields.shape, bf16),
            dma,
            dma((blocks,)),
            dma((blocks,)),
        ],
        compiler_params=pltpu.CompilerParams(vmem_limit_bytes=60 * 1024 * 1024),
    )(restore_table(each), returned)


def solution(mesh):
    return jax.shard_map(
        shards,
        mesh=mesh,
        in_specs=(P(None, "wide", "narrow", None), P("wide"), P("wide"), P()),
        out_specs=P(None, "wide", "narrow", None),
        check_vma=False,
    )
```

```python
import functools

import jax
import jax.numpy as jnp
import numpy as np
from jax import lax
from jax.experimental import pallas as pl
from jax.experimental.pallas import tpu as pltpu
from jax.sharding import PartitionSpec as P

time_step = 0.02
lift_gain = 24.0
upwind_share = 0.5
GROUP = 16
CHUNK = 128
TILE = 256
MESH = pl.DeviceIdType.MESH


def derivative_matrix():
    points_ref = -np.cos(np.pi * np.arange(8) / 7.0)
    identity = np.eye(8)
    differ = points_ref[:, None] - points_ref[None, :] + identity
    weights = 1.0 / np.prod(differ, axis=1)
    derivative = weights[None, :] / weights[:, None] / differ * (1.0 - identity)
    return derivative - identity * derivative.sum(axis=1)[:, None]


def as_table(matrix):
    return jnp.asarray(matrix, dtype=jnp.float32).astype(jnp.bfloat16)


def lane_tables():
    derivative = derivative_matrix()
    along_x = np.kron(np.eye(2), np.kron(derivative, np.eye(8)))
    along_y = np.kron(np.eye(2), np.kron(np.eye(8), derivative))
    slopes = np.concatenate([along_x.T, along_y.T], axis=1)
    lane = np.arange(CHUNK)
    p, q = lane // 8 % 8, lane % 8
    faces_x = np.zeros((2 * CHUNK, CHUNK))
    first, last = lane[p == 0], lane[p == 7]
    faces_x[first + 56, first] = 1.0
    faces_x[CHUNK + last - 56, last] = 1.0
    faces_y = np.zeros((3 * CHUNK, CHUNK))
    for target in lane[q == 0]:
        source = target - 57
        faces_y[source if source >= 0 else 2 * CHUNK + source, target] = 1.0
    for target in lane[q == 7]:
        source = target + 57
        faces_y[source if source < CHUNK else CHUNK + source, target] = 1.0
    return slopes, faces_x, faces_y


def swap_table():
    row = np.arange(GROUP * GROUP)
    table = np.zeros((GROUP * GROUP, GROUP * GROUP))
    table[row, row % GROUP * GROUP + row // GROUP] = 1.0
    return table


def joined_tables():
    slopes, faces_x, faces_y = lane_tables()
    faces = np.zeros((3 * CHUNK, TILE))
    faces[:, :CHUNK] = faces_y
    faces[: 2 * CHUNK, CHUNK:] = faces_x
    return as_table(np.concatenate([swap_table(), slopes, faces], axis=0))


def restore_table(each):
    owners = GROUP // each
    v, column = np.meshgrid(np.arange(GROUP), np.arange(GROUP), indexing="ij")
    source = (column % each * owners + column // each) * GROUP + v
    table = np.zeros((GROUP * GROUP, GROUP * GROUP))
    table[(v * GROUP + column).ravel(), source.ravel()] = 1.0
    return as_table(table)


def sweep_kernel(
    n, strips, each,
    fields_in, vel_x_in, vel_y_in, collision_in, tables_in,
    result,
    fields, vel_x, vel_y, collision, tables, columns, packed, gathered, mixed, coefs,
    edge_send, edge_recv, out_send, out_recv, back_send, back_recv, own_sem, load_sem,
):
    me = lax.axis_index("wide")
    strip = lax.axis_index("narrow")
    pairs, local, width, lanes = fields.shape
    rows = pairs * local
    speeds = n * local
    chunks = lanes // CHUNK
    groups = local // GROUP
    swap = tables.at[pl.ds(0, TILE), :]
    slopes = tables.at[pl.ds(TILE, CHUNK), :]
    faces_y = tables.at[pl.ds(TILE + CHUNK, 3 * CHUNK), pl.ds(0, CHUNK)]
    faces_x = tables.at[pl.ds(TILE + CHUNK, 2 * CHUNK), pl.ds(CHUNK, CHUNK)]
    loads = [pltpu.make_async_copy(tables_in, tables, load_sem.at[0])]
    for s in range(pairs):
        for g in range(groups):
            part = (s, pl.ds(g * GROUP, GROUP))
            loads.append(
                pltpu.make_async_copy(
                    fields_in.at[part], fields.at[part], load_sem.at[1 + s * groups + g]
                )
            )
    for k, (source, target) in enumerate(
        ((vel_x_in, vel_x), (vel_y_in, vel_y), (collision_in, collision))
    ):
        loads.append(
            pltpu.make_async_copy(source, target, load_sem.at[1 + pairs * groups + k])
        )
    for load in (*loads[-3:-1], *loads[:-3], loads[-1]):
        load.start()
    above, below = lax.rem(strip + 1, strips), lax.rem(strip + strips - 1, strips)

    half = n // 2
    upper, place = me // half, lax.rem(me, half)

    def partner(i):
        near = i // half
        return lax.rem(upper + 1 - near, 2) * half + lax.rem(place + i + near, half)

    barrier = pltpu.get_barrier_semaphore()

    def greet(i, carry):
        pl.semaphore_signal(
            barrier, inc=1, device_id={"wide": lax.rem(me + i, n)}, device_id_type=MESH
        )
        return carry

    lax.fori_loop(1, n, greet, 0)
    for neighbour in (above, below):
        pl.semaphore_signal(barrier, inc=1, device_id={"narrow": neighbour}, device_id_type=MESH)

    lane = lax.broadcasted_iota(jnp.int32, (rows, CHUNK), 1)
    node_p = (lane >> 3) & 7
    node_q = lane & 7
    eye = lax.broadcasted_iota(jnp.int32, (local, local), 0) == lax.broadcasted_iota(
        jnp.int32, (local, local), 1
    )

    def signed(vel):
        spread = jnp.broadcast_to(vel[...], (local, local))
        column = jnp.sum(jnp.where(eye, spread, 0.0), axis=1, keepdims=True)
        return jnp.broadcast_to(jnp.concatenate([column, -column], axis=0), (rows, CHUNK))

    loads[-3].wait()
    loads[-2].wait()
    lift = time_step * lift_gain
    own = jnp.ones((rows, CHUNK), jnp.float32)
    for k, (speed, node) in enumerate(((signed(vel_x), node_p), (signed(vel_y), node_q))):
        plus = 0.5 * (speed + upwind_share * jnp.abs(speed))
        minus = 0.5 * (speed - upwind_share * jnp.abs(speed))
        face = lift * (jnp.where(node == 0, plus, 0.0) - jnp.where(node == 7, minus, 0.0))
        own = own - face
        coefs[1 + k] = -time_step * speed
        coefs[3 + k] = face
    coefs[0] = own

    loads[0].wait()
    for s in range(pairs):
        for g in range(groups):
            loads[1 + s * groups + g].wait()
            for h in range(width // GROUP):
                at = h * GROUP
                for t in range(lanes // TILE):
                    part = pl.ds(t * TILE, TILE)
                    block = fields[s, pl.ds(g * GROUP, GROUP), pl.ds(at, GROUP), part]
                    turned = jnp.dot(
                        swap[...], block.reshape(GROUP * GROUP, TILE),
                        preferred_element_type=jnp.float32,
                    )
                    columns[
                        pl.ds(at + 1, GROUP), pl.ds(s * local + g * GROUP, GROUP), part
                    ] = turned.astype(jnp.bfloat16).reshape(GROUP, GROUP, TILE)

    pl.semaphore_wait(barrier, n + 1)

    def edge(k):
        source, target, device = ((width, 0, above), (1, width + 1, below))[k]
        return pltpu.make_async_remote_copy(
            src_ref=columns.at[source], dst_ref=columns.at[target],
            send_sem=edge_send.at[k], recv_sem=edge_recv.at[k],
            device_id={"narrow": device}, device_id_type=MESH,
        )

    edge(0).start()
    edge(1).start()

    def outward(c, d, at):
        return pltpu.make_async_remote_copy(
            src_ref=packed.at[c, d],
            dst_ref=gathered.at[c, :, pl.ds(pl.multiple_of(at * local, GROUP), local), :],
            send_sem=out_send.at[c, d], recv_sem=out_recv.at[c, at],
            device_id={"wide": d}, device_id_type=MESH,
        )

    def stacked(value, shift):
        return jnp.concatenate(
            [
                value[:, (m + shift) % chunks * CHUNK : ((m + shift) % chunks + 1) * CHUNK]
                for m in range(chunks)
            ],
            axis=0,
        )

    for c in range(each):
        def transport(i, carry):
            d = partner(i)
            if c == 0:
                @pl.when(d == 0)
                def _():
                    edge(0).wait_recv()
            if c == each - 1:
                @pl.when(d == n - 1)
                def _():
                    edge(1).wait_recv()
            j = d * each + c
            now = columns[j + 1]
            here = stacked(now, 0)
            slope = jnp.dot(here, slopes[...], preferred_element_type=jnp.float32)
            next_x = jnp.dot(
                jnp.concatenate([stacked(columns[j], 0), stacked(columns[j + 2], 0)], axis=1),
                faces_x[...], preferred_element_type=jnp.float32,
            )
            next_y = jnp.dot(
                jnp.concatenate([here, stacked(now, -1), stacked(now, 1)], axis=1),
                faces_y[...], preferred_element_type=jnp.float32,
            )
            for m in range(chunks):
                span = slice(m * rows, (m + 1) * rows)
                moved = (
                    coefs[0] * here[span].astype(jnp.float32)
                    + coefs[1] * slope[span, :CHUNK]
                    + coefs[2] * slope[span, CHUNK:]
                    + coefs[3] * next_x[span]
                    + coefs[4] * next_y[span]
                )
                packed[c, d, :, :, pl.ds(m * CHUNK, CHUNK)] = moved.astype(jnp.bfloat16).reshape(
                    pairs, local, CHUNK
                )

            @pl.when(i < n - 1)
            def _():
                outward(c, d, me).start()

            return carry

        lax.fori_loop(0, n, transport, 0)
        pltpu.make_async_copy(
            packed.at[c, me],
            gathered.at[c, :, pl.ds(pl.multiple_of(me * local, GROUP), local), :],
            own_sem.at[c],
        ).start()

    def back(c, d, at):
        return pltpu.make_async_remote_copy(
            src_ref=mixed.at[c, d], dst_ref=result.at[c, at],
            send_sem=back_send.at[c, d], recv_sem=back_recv.at[c, at],
            device_id={"wide": d}, device_id_type=MESH,
        )

    loads[-1].wait()
    for c in range(each):
        pltpu.make_async_copy(
            packed.at[c, me],
            gathered.at[c, :, pl.ds(pl.multiple_of(me * local, GROUP), local), :],
            own_sem.at[c],
        ).wait()

        def arrive(i, carry):
            d = lax.rem(me + n - i, n)
            outward(c, d, d).wait_recv()
            return carry

        lax.fori_loop(1, n, arrive, 0)

        def collide(i, carry):
            d = partner(i)
            left = jnp.concatenate(
                [
                    collision[pl.ds(pl.multiple_of(s * speeds + d * local, GROUP), local), :]
                    for s in range(pairs)
                ],
                axis=0,
            )
            for t in range(lanes // TILE):
                part = pl.ds(t * TILE, TILE)
                total = jnp.dot(
                    left, gathered[c, :, :, part].reshape(pairs * speeds, TILE),
                    preferred_element_type=jnp.float32,
                )
                mixed[c, d, :, :, part] = total.astype(jnp.bfloat16).reshape(pairs, local, TILE)

            @pl.when(i < n - 1)
            def _():
                back(c, d, me).start()

            return carry

        lax.fori_loop(0, n, collide, 0)
        pltpu.make_async_copy(
            mixed.at[c, me], result.at[c, me], own_sem.at[each + c]
        ).start()

    edge(0).wait_send()
    edge(1).wait_send()
    for c in range(each):
        pltpu.make_async_copy(
            mixed.at[c, me], result.at[c, me], own_sem.at[each + c]
        ).wait()

        def finish(i, carry):
            d = lax.rem(me + i, n)
            outward(c, d, me).wait_send()
            back(c, d, me).wait_send()
            back(c, d, d).wait_recv()
            return carry

        lax.fori_loop(1, n, finish, 0)


def restore_kernel(table_in, returned, result, table, held, turned, table_sem, in_sem, out_sem):
    each, n, pairs, local, lanes = held.shape
    owners = GROUP // each
    blocks = [
        (s, g, h)
        for s in range(pairs)
        for g in range(local // GROUP)
        for h in range(n // owners)
    ]

    def fetch(k):
        s, g, h = blocks[k]
        part = (slice(None), pl.ds(h * owners, owners), s, pl.ds(g * GROUP, GROUP))
        return pltpu.make_async_copy(returned.at[part], held.at[part], in_sem.at[k])

    def place(k):
        s, g, h = blocks[k]
        part = (s, pl.ds(g * GROUP, GROUP), pl.ds(h * GROUP, GROUP))
        return pltpu.make_async_copy(turned.at[part], result.at[part], out_sem.at[k])

    load = pltpu.make_async_copy(table_in, table, table_sem)
    load.start()
    for k in range(len(blocks)):
        fetch(k).start()
    load.wait()
    for k, (s, g, h) in enumerate(blocks):
        fetch(k).wait()
        for t in range(lanes // TILE):
            part = pl.ds(t * TILE, TILE)
            block = held[:, pl.ds(h * owners, owners), s, pl.ds(g * GROUP, GROUP), part]
            rows = jnp.dot(
                table[...], block.reshape(GROUP * GROUP, TILE),
                preferred_element_type=jnp.float32,
            )
            turned[s, pl.ds(g * GROUP, GROUP), pl.ds(h * GROUP, GROUP), part] = rows.astype(
                jnp.bfloat16
            ).reshape(GROUP, GROUP, TILE)
        place(k).start()
    for k in range(len(blocks)):
        place(k).wait()


def shards(fields, vel_x, vel_y, collision):
    n = lax.axis_size("wide")
    strips = lax.axis_size("narrow")
    pairs, local, width, lanes = fields.shape
    each = width // n
    rows = pairs * local
    bf16 = jnp.bfloat16
    hbm = pl.BlockSpec(memory_space=pltpu.HBM)
    dma = pltpu.SemaphoreType.DMA
    returned = pl.pallas_call(
        functools.partial(sweep_kernel, n, strips, each),
        out_shape=jax.ShapeDtypeStruct((each, n, pairs, local, lanes), bf16),
        in_specs=[hbm] * 5,
        out_specs=hbm,
        scratch_shapes=[
            pltpu.VMEM(fields.shape, bf16),
            pltpu.VMEM((1, local), jnp.float32),
            pltpu.VMEM((1, local), jnp.float32),
            pltpu.VMEM(collision.shape, bf16),
            pltpu.VMEM((2 * TILE + 2 * CHUNK, TILE), bf16),
            pltpu.VMEM((width + 2, rows, lanes), bf16),
            pltpu.VMEM((each, n, pairs, local, lanes), bf16),
            pltpu.VMEM((each, pairs, n * local, lanes), bf16),
            pltpu.VMEM((each, n, pairs, local, lanes), bf16),
            pltpu.VMEM((5, rows, CHUNK), jnp.float32),
            dma((2,)),
            dma((2,)),
            dma((each, n)),
            dma((each, n)),
            dma((each, n)),
            dma((each, n)),
            dma((2 * each,)),
            dma((4 + pairs * (local // GROUP),)),
        ],
        compiler_params=pltpu.CompilerParams(
            collective_id=0, has_side_effects=True, vmem_limit_bytes=62 * 1024 * 1024
        ),
    )(
        fields, vel_x.reshape(1, local), vel_y.reshape(1, local), collision,
        joined_tables(),
    )
    blocks = pairs * (local // GROUP) * (width // GROUP)
    return pl.pallas_call(
        restore_kernel,
        out_shape=jax.ShapeDtypeStruct(fields.shape, bf16),
        in_specs=[hbm] * 2,
        out_specs=hbm,
        scratch_shapes=[
            pltpu.VMEM((GROUP * GROUP, GROUP * GROUP), bf16),
            pltpu.VMEM((each, n, pairs, local, lanes), bf16),
            pltpu.VMEM(fields.shape, bf16),
            dma,
            dma((blocks,)),
            dma((blocks,)),
        ],
        compiler_params=pltpu.CompilerParams(vmem_limit_bytes=60 * 1024 * 1024),
    )(restore_table(each), returned)


def solution(mesh):
    return jax.shard_map(
        shards,
        mesh=mesh,
        in_specs=(P(None, "wide", "narrow", None), P("wide"), P("wide"), P()),
        out_specs=P(None, "wide", "narrow", None),
        check_vma=False,
    )
```
